32 devices in a mesh: group: 4 (over z), tp: 8 (over y, x, core).
Axes of the slice: x: 2, y: 2, z: 4, core: 2. Of those that a mesh axis runs over, the one named last changes fastest.
Arguments:
- tokens: bfloat16 [2048, 4096], P('group', 'tp'), may hold values from -6 to 6
- route_ids: int32 [2048, 2], P('group'), may hold values from 0 to 3, all different within a row; in each aligned block of 512 rows (0 to 511, 512 to 1023, ...) at most 320 rows name the same one
- route_weight: float32 [2048, 2], P('group'), may hold values from 0.25 to 4
- gate_weight: bfloat16 [4096, 6144], P(None, 'tp'), may hold values from -0.09375 to 0.09375
- up_weight: bfloat16 [4096, 6144], P(None, 'tp'), may hold values from -0.09375 to 0.09375
- down_weight: bfloat16 [6144, 4096], P('tp'), may hold values from -0.15625 to 0.15625
- gate_code: bfloat16 [4096, 6144], P('group', 'tp'), may hold values from -1 to 1
- up_code: bfloat16 [4096, 6144], P('group', 'tp'), may hold values from -1 to 1
- gate_scale: bfloat16 [32, 6144], P('group', 'tp'), may hold values from 0.0049743652 to 0.049804688
- up_scale: bfloat16 [32, 6144], P('group', 'tp'), may hold values from 0.0049743652 to 0.049804688
- down_code: bfloat16 [6144, 4096], P('tp', 'group'), may hold values from -1 to 1
- down_scale: bfloat16 [6144, 32], P('tp', 'group'), may hold values from 0.0079956055 to 0.079589844
Outputs:
- decoded: bfloat16 [2048, 4096], P('group', 'tp')
The draws below stay inside these ranges and needn't reach their ends.
Inputs may be any that keep to these rules, and one draw needn't show every extreme that they name: `route_ids`: each token names 2 different experts; among the 512 tokens of one group no expert is named by more than 320 tokens.
All inputs are finite; a program needn't handle non-finite values.
Results may differ from the reference program's by a relative error of at most 0.007.
Values may be sent and summed in bfloat16 or wider, within the bound.
A program may use at most 128 MiB of HBM per device.

```python
import math
import jax
import jax.numpy as jnp
import numpy as np

D = 4096
FF = 1536
EXPERTS = 4
TOPK = 2
BLOCK = 128
ROWS = 512
TOKENS = 2048
CAP = 320


def level_of(key, dims, shards, least, high):
    def one(axis_at, parts):
        heights = jax.random.uniform(jax.random.fold_in(jax.random.fold_in(key, 6), axis_at), (parts,), jnp.float32, least / len(shards), high / len(shards))
        return jnp.repeat(jnp.exp(heights), dims[axis_at] // parts).reshape((-1,) + (1,) * (len(dims) - axis_at - 1))

    factor_of = one(*shards[0])
    for cut in shards[1:]:
        factor_of = factor_of * one(*cut)
    return factor_of


def routed_block(rng, own, number, rows, count, top, bound, lean):
    ranking = jax.random.permutation(rng, count)
    heavy_load, usual = load_shares(count, rows * top, bound, lean, True), load_shares(count, rows * top, bound, lean, False)
    places = jnp.arange(count)

    def named(sizes, offset_by):
        used = int((sizes > 0).sum())
        fixed = max(1, used // 4)
        passed = fixed + (places - fixed + offset_by * (used - fixed)) % max(1, count - fixed)
        return jnp.zeros((count,), jnp.int32).at[ranking[jnp.where(places < fixed, places, passed)]].set(jnp.asarray(sizes, jnp.int32))

    sizes = jnp.where(number % 4 == 0, named(heavy_load, number // 4), named(usual, number - number // 4 - 1))
    mixed = jax.random.permutation(jax.random.fold_in(own, 3), count)
    donor, sink = mixed[0:count // 2 * 2:2], mixed[1:count // 2 * 2:2]
    slack = jnp.minimum(sizes[donor] - 1, bound - sizes[sink]) // 2
    slack = jnp.where((donor == ranking[0]) | (sink == ranking[0]) | (sizes[sink] == 0), 0, jnp.maximum(slack, 0))
    passed = jax.random.randint(jax.random.fold_in(own, 4), (count // 2,), 0, 1 << 20) % (slack + 1)
    sizes = sizes.at[donor].add(-passed).at[sink].add(passed)
    labels = jnp.searchsorted(jnp.cumsum(sizes), jnp.arange(rows * top), side="right").astype(jnp.int32)
    grid = labels.reshape(top, rows).T
    grid = grid[jax.random.permutation(jax.random.fold_in(own, 1), rows)]
    offset_by = jax.random.randint(jax.random.fold_in(own, 2), (rows, 1), 0, top)
    return jnp.take_along_axis(grid, (jnp.arange(top)[None, :] + offset_by) % top, axis=1)


def load_shares(number_of, total, bound, lean, full):
    portions = [(1 << 20) // math.isqrt(standing ** lean) + 1 for standing in range(1, number_of + 1)]
    largest = bound if full else min(bound, max(-(-total // number_of), total * portions[0] // sum(portions)))
    least = 1 if total - largest >= number_of - 1 else 0
    holding, spare = [largest] + [least] * (number_of - 1), total - largest - least * (number_of - 1)
    while spare > 0:
        movable = [i for i in range(1, number_of) if holding[i] < largest] or [i for i in range(1, number_of) if holding[i] < bound]
        mass, budget = sum([portions[i] for i in movable]), spare
        for i in movable:
            addition = min(bound - holding[i], max(1, budget * portions[i] // mass), spare)
            holding[i] = holding[i] + addition
            spare = spare - addition
    return np.array(holding)


def scatter_about(stream_key, dims, scale, most, shards=(), kind=jnp.bfloat16):
    values = jax.random.normal(stream_key, dims, jnp.float32) * scale
    if len(shards) > 0:
        values = level_of(stream_key, dims, shards, -0.22, 0.18) * values
    return jnp.clip(values, min=-most, max=most).astype(kind)


def setup_inputs(seed: int = 0) -> dict:
    key_of = jax.random.split(jax.random.key(seed), 13)
    tokens = scatter_about(key_of[0], (TOKENS, D), 1.0, 6.0, ((0, 4), (1, 8)))
    route_ids_keys = jax.random.split(jax.random.fold_in(key_of[1], 1), TOKENS // ROWS)
    route_ids_turns = jax.random.permutation(jax.random.fold_in(key_of[1], 3), TOKENS // ROWS)
    route_ids = jax.vmap(lambda own, number: routed_block(jax.random.fold_in(key_of[1], 2), own, number, ROWS, EXPERTS, TOPK, CAP, 1))(route_ids_keys, route_ids_turns).reshape((TOKENS, TOPK))
    route_weight = jnp.clip(jnp.exp(math.log(4.0) - 2.7725887 * jax.random.uniform(key_of[2], (TOKENS, TOPK), jnp.float32) ** level_of(key_of[2], (TOKENS, TOPK), ((0, 4),), -0.2, 0.2)), 0.25, 4.0)
    gate_weight = scatter_about(key_of[3], (D, EXPERTS * FF), D ** -0.5, 0.09375, ((1, 8),))
    up_weight = scatter_about(key_of[4], (D, EXPERTS * FF), D ** -0.5, 0.09375, ((1, 8),))
    down_weight = scatter_about(key_of[5], (EXPERTS * FF, D), FF ** -0.5, 0.15625, ((0, 8),))
    gate_code = jnp.clip(jax.random.uniform(key_of[6], (D, EXPERTS * FF), jnp.float32, -1.0, 1.0) * level_of(key_of[6], (D, EXPERTS * FF), ((0, 4), (1, 8)), -0.4, 0.0), -1.0, 1.0).astype(jnp.bfloat16)
    up_code = jnp.clip(jax.random.uniform(key_of[7], (D, EXPERTS * FF), jnp.float32, -1.0, 1.0) * level_of(key_of[7], (D, EXPERTS * FF), ((0, 4), (1, 8)), -0.4, 0.0), -1.0, 1.0).astype(jnp.bfloat16)
    gate_scale = jnp.clip(jnp.exp(math.log(0.049804688) - 2.3038113 * jax.random.uniform(key_of[8], (D // BLOCK, EXPERTS * FF), jnp.float32) ** level_of(key_of[8], (D // BLOCK, EXPERTS * FF), ((0, 4), (1, 8)), -0.2, 0.2)), 0.0049743652, 0.049804688).astype(jnp.bfloat16)
    up_scale = jnp.clip(jnp.exp(math.log(0.049804688) - 2.3038113 * jax.random.uniform(key_of[9], (D // BLOCK, EXPERTS * FF), jnp.float32) ** level_of(key_of[9], (D // BLOCK, EXPERTS * FF), ((0, 4), (1, 8)), -0.2, 0.2)), 0.0049743652, 0.049804688).astype(jnp.bfloat16)
    down_code = jnp.clip(jax.random.uniform(key_of[10], (EXPERTS * FF, D), jnp.float32, -1.0, 1.0) * level_of(key_of[10], (EXPERTS * FF, D), ((0, 8), (1, 4)), -0.4, 0.0), -1.0, 1.0).astype(jnp.bfloat16)
    down_scale = jnp.clip(jnp.exp(math.log(0.079589844) - 2.2979944 * jax.random.uniform(key_of[11], (EXPERTS * FF, D // BLOCK), jnp.float32) ** level_of(key_of[11], (EXPERTS * FF, D // BLOCK), ((0, 8), (1, 4)), -0.2, 0.2)), 0.0079956055, 0.079589844).astype(jnp.bfloat16)
    return {"tokens": tokens, "route_ids": route_ids, "route_weight": route_weight, "gate_weight": gate_weight, "up_weight": up_weight, "down_weight": down_weight, "gate_code": gate_code, "up_code": up_code, "gate_scale": gate_scale, "up_scale": up_scale, "down_code": down_code, "down_scale": down_scale}


def refresh_rows(weight, code, scale):
    width = weight.shape[1]
    delta = code.astype(jnp.float32).reshape(scale.shape[0], -1, width) * scale.astype(jnp.float32)[:, None, :]
    return (weight.astype(jnp.float32) + delta.reshape(weight.shape)).astype(jnp.bfloat16)


def refresh_cols(weight, code, scale):
    height = weight.shape[0]
    delta = code.astype(jnp.float32).reshape(height, scale.shape[1], -1) * scale.astype(jnp.float32)[:, :, None]
    return (weight.astype(jnp.float32) + delta.reshape(weight.shape)).astype(jnp.bfloat16)


def reference(tokens, route_ids, route_weight, gate_weight, up_weight, down_weight, gate_code, up_code, gate_scale, up_scale, down_code, down_scale):
    gate_new = refresh_rows(gate_weight, gate_code, gate_scale)
    up_new = refresh_rows(up_weight, up_code, up_scale)
    down_new = refresh_cols(down_weight, down_code, down_scale)
    combine = route_weight / jnp.sum(route_weight, axis=1, keepdims=True)
    total = jnp.zeros((tokens.shape[0], tokens.shape[1]), jnp.float32)
    for expert in range(EXPERTS):
        start = expert * FF
        gate_value = jnp.dot(tokens, gate_new[:, start:start + FF], preferred_element_type=jnp.float32)
        up_value = jnp.dot(tokens, up_new[:, start:start + FF], preferred_element_type=jnp.float32)
        hidden = (jax.nn.silu(gate_value) * up_value).astype(jnp.bfloat16)
        result = jnp.dot(hidden, down_new[start:start + FF, :], preferred_element_type=jnp.float32)
        weight_row = jnp.sum(jnp.where(route_ids == expert, combine, jnp.zeros_like(combine)), axis=1)
        total = total + weight_row[:, None] * result
    return total.astype(jnp.bfloat16)
```

```python
import jax
import jax.numpy as jnp
from jax import lax
from jax.sharding import PartitionSpec as P

EXPERTS = 4


def refresh_rows(weight, code, scale):
    width = weight.shape[1]
    delta = (
        code.astype(jnp.float32).reshape(scale.shape[0], -1, width)
        * scale.astype(jnp.float32)[:, None, :]
    )
    return (weight.astype(jnp.float32) + delta.reshape(weight.shape)).astype(jnp.bfloat16)


def refresh_cols(weight, code, scale):
    height = weight.shape[0]
    delta = (
        code.astype(jnp.float32).reshape(height, scale.shape[1], -1)
        * scale.astype(jnp.float32)[:, :, None]
    )
    return (weight.astype(jnp.float32) + delta.reshape(weight.shape)).astype(jnp.bfloat16)


def body(
    tokens,
    route_ids,
    route_weight,
    gate_weight,
    up_weight,
    down_weight,
    gate_code,
    up_code,
    gate_scale,
    up_scale,
    down_code,
    down_scale,
):
    groups, share = lax.axis_size("group"), lax.axis_size("tp")
    group = lax.axis_index("group")
    rows, part = tokens.shape
    width = part * share
    depth = width // groups
    columns = down_code.shape[1]
    capacity = rows * route_ids.shape[1] * 5 // (EXPERTS * 4)
    expert = lax.axis_index("tp") // (share // EXPERTS)

    mine = lax.all_to_all(tokens, "tp", split_axis=0, concat_axis=1, tiled=True)
    mine = mine.reshape(rows // share, groups, depth).transpose(1, 0, 2)
    mine = lax.all_to_all(mine, "group", split_axis=0, concat_axis=0, tiled=True)
    every = lax.all_gather(mine, "tp", axis=1, tiled=True)

    combine = route_weight / jnp.sum(route_weight, axis=1, keepdims=True)
    named = route_ids == expert
    weight_row = jnp.sum(jnp.where(named, combine, jnp.zeros_like(combine)), axis=1)
    used = jnp.any(named, axis=1)
    place = jnp.cumsum(used.astype(jnp.int32)) - 1
    target = jnp.where(used, place, capacity)
    both = jnp.stack([target.astype(jnp.float32), weight_row], axis=0)
    both = lax.all_gather(both, "group", axis=0, tiled=False)
    target_all = both[:, 0].astype(jnp.int32)
    pick = target_all[:, None, :] == lax.broadcasted_iota(jnp.int32, (groups, capacity, rows), 1)
    slot_weight = jnp.sum(jnp.where(pick, both[:, 1][:, None, :], 0.0), axis=2)
    pick = pick.astype(jnp.bfloat16)

    picked = jnp.einsum("gsn,gnk->gsk", pick, every)
    picked = picked.reshape(groups * capacity, depth)

    gate_new = refresh_rows(
        lax.dynamic_slice_in_dim(gate_weight, group * depth, depth, 0), gate_code, gate_scale
    )
    up_new = refresh_rows(
        lax.dynamic_slice_in_dim(up_weight, group * depth, depth, 0), up_code, up_scale
    )
    down_new = refresh_cols(
        lax.dynamic_slice_in_dim(down_weight, group * columns, columns, 1), down_code, down_scale
    )
    both_new = jnp.concatenate([gate_new, up_new], axis=1)
    value = jnp.dot(picked, both_new, preferred_element_type=jnp.float32).astype(jnp.bfloat16)
    value = value.reshape(groups, capacity, -1)
    value = lax.all_to_all(value, "group", split_axis=0, concat_axis=0, tiled=True)
    value = jnp.sum(value.astype(jnp.float32), axis=0)
    half = value.shape[1] // 2
    hidden = (jax.nn.silu(value[:, :half]) * value[:, half:]).astype(jnp.bfloat16)

    hidden_all = lax.all_gather(hidden, "group", axis=0, tiled=True)
    term = jnp.dot(hidden_all, down_new, preferred_element_type=jnp.float32)
    term = (term.reshape(groups, capacity, columns) * slot_weight[:, :, None]).astype(jnp.bfloat16)
    spread = jnp.einsum("gsn,gsk->gnk", pick, term)
    spread = spread.reshape(groups, share, rows // share, columns).transpose(1, 0, 2, 3)
    total = lax.psum_scatter(spread, "tp", scatter_dimension=0, tiled=True)[0]
    total = lax.all_to_all(total, "group", split_axis=0, concat_axis=0, tiled=True)
    total = total.transpose(1, 0, 2).reshape(rows // share, width)
    return lax.all_to_all(total, "tp", split_axis=1, concat_axis=0, tiled=True).astype(jnp.bfloat16)


def solution(mesh):
    placed = (
        P("group", "tp"),
        P("group", None),
        P("group", None),
        P(None, "tp"),
        P(None, "tp"),
        P("tp", None),
        P("group", "tp"),
        P("group", "tp"),
        P("group", "tp"),
        P("group", "tp"),
        P("tp", "group"),
        P("tp", "group"),
    )
    return jax.shard_map(
        body, mesh=mesh, in_specs=placed, out_specs=P("group", "tp"), check_vma=False
    )
```

```python
import functools

import jax
import jax.numpy as jnp
from jax import lax
from jax.experimental import pallas as pl
from jax.experimental.pallas import tpu as pltpu
from jax.sharding import PartitionSpec as P

EXPERTS = 4
CHUNK = 64


def expert_kernel(
    groups,
    chunk,
    x_ref,
    w_ref,
    down_ref,
    weight_ref,
    term_ref,
    out_up,
    out_low,
    in_up,
    in_low,
    hidden,
    sem,
):
    me = lax.axis_index("group")
    last = groups - 1
    half = x_ref.shape[0] // 2
    count = half // chunk
    width = w_ref.shape[1] // 2

    barrier = pltpu.get_barrier_semaphore()

    @pl.when(me > 0)
    def _():
        pl.semaphore_signal(
            barrier, inc=1, device_id={"group": me - 1}, device_id_type=pl.DeviceIdType.MESH
        )

    @pl.when(me < last)
    def _():
        pl.semaphore_signal(
            barrier, inc=1, device_id={"group": me + 1}, device_id_type=pl.DeviceIdType.MESH
        )

    @pl.when((me > 0) & (me < last))
    def _():
        pl.semaphore_wait(barrier, 2)

    @pl.when((me == 0) | (me == last))
    def _():
        pl.semaphore_wait(barrier, 1)

    def piece(k, start):
        return pl.ds(pl.multiple_of(start + k * chunk, chunk), chunk)

    def move(k, source, target, number, where):
        return pltpu.make_async_remote_copy(
            src_ref=source,
            dst_ref=target,
            send_sem=sem.at[number, k],
            recv_sem=sem.at[number + 1, k],
            device_id={"group": where},
            device_id_type=pl.DeviceIdType.MESH,
        )

    def sum_move(k, upward):
        if upward:
            return move(k, out_up.at[piece(k, 0)], in_up.at[piece(k, 0)], 0, lax.rem(me + 1, groups))
        return move(k, out_low.at[piece(k, 0)], in_low.at[piece(k, 0)], 2, lax.rem(me + last, groups))

    def hidden_move(k, upward):
        if upward:
            return move(k, hidden.at[piece(k, half)], hidden.at[piece(k, half)], 4, lax.rem(me + last, groups))
        return move(k, hidden.at[piece(k, 0)], hidden.at[piece(k, 0)], 6, lax.rem(me + 1, groups))

    def finish(k, start):
        rows = piece(k, start)
        term = jnp.dot(hidden[rows, :], down_ref[...], preferred_element_type=jnp.float32)
        term_ref[rows, :] = (term * weight_ref[rows, :]).astype(jnp.bfloat16)

    def add(k, upward):
        start = half if upward else 0
        first, final = (0, last) if upward else (last, 0)
        inside, outside = (in_up, out_up) if upward else (in_low, out_low)
        here = piece(k, 0)
        own = jnp.dot(x_ref[piece(k, start), :], w_ref[...], preferred_element_type=jnp.float32)

        @pl.when(me == first)
        def _():
            outside[here, :] = own.astype(jnp.bfloat16)

        @pl.when(me != first)
        def _():
            sum_move(k, upward).wait_recv()

            @pl.when(me != final)
            def _():
                outside[here, :] = (own + inside[here, :].astype(jnp.float32)).astype(jnp.bfloat16)

            @pl.when(me == final)
            def _():
                value = own + inside[here, :].astype(jnp.float32)
                gate, up = value[:, :width], value[:, width:]
                hidden[piece(k, start), :] = (gate / (1.0 + jnp.exp(-gate)) * up).astype(
                    jnp.bfloat16
                )

        @pl.when(me != final)
        def _():
            sum_move(k, upward).start()

        @pl.when(me == final)
        def _():
            hidden_move(k, upward).start()
            finish(k, start)

    def take(k, upward):
        final, end = (last, 0) if upward else (0, last)
        hidden_move(k, upward).wait_recv()

        @pl.when(me != end)
        def _():
            hidden_move(k, upward).start()

        finish(k, half if upward else 0)

    def step(t, _):
        for upward in (True, False):
            place = me if upward else last - me
            k = t - place

            @pl.when((k >= 0) & (k < count))
            def _():
                add(k, upward)

        for upward in (True, False):
            place = me if upward else last - me
            j = t - (2 * last - place)

            @pl.when((j >= 0) & (j < count) & (place != last))
            def _():
                take(j, upward)

        return 0

    lax.fori_loop(0, count + 2 * last, step, 0)

    def settle(k, _):
        for upward in (True, False):
            final, end = (last, 0) if upward else (0, last)

            @pl.when(me != final)
            def _():
                sum_move(k, upward).wait_send()

            @pl.when(me != end)
            def _():
                hidden_move(k, upward).wait_send()

        return 0

    lax.fori_loop(0, count, settle, 0)


def expert_terms(groups, picked, both_new, down_new, slot_weight):
    rows, columns = picked.shape[0], down_new.shape[1]
    half, width = rows // 2, down_new.shape[0]
    chunk = CHUNK
    vmem = pl.BlockSpec(memory_space=pltpu.VMEM)
    return pl.pallas_call(
        functools.partial(expert_kernel, groups, chunk),
        out_shape=jax.ShapeDtypeStruct((rows, columns), jnp.bfloat16),
        in_specs=[vmem] * 4,
        out_specs=vmem,
        scratch_shapes=[
            *[pltpu.VMEM((half, 2 * width), jnp.bfloat16)] * 4,
            pltpu.VMEM((rows, width), jnp.bfloat16),
            pltpu.SemaphoreType.DMA((8, half // chunk)),
        ],
        compiler_params=pltpu.CompilerParams(
            collective_id=0, has_side_effects=True, vmem_limit_bytes=48 * 1024 * 1024
        ),
    )(picked, both_new, down_new, slot_weight)


def refresh_rows(weight, code, scale):
    width = weight.shape[1]
    delta = (
        code.astype(jnp.float32).reshape(scale.shape[0], -1, width)
        * scale.astype(jnp.float32)[:, None, :]
    )
    return (weight.astype(jnp.float32) + delta.reshape(weight.shape)).astype(jnp.bfloat16)


def refresh_cols(weight, code, scale):
    height = weight.shape[0]
    delta = (
        code.astype(jnp.float32).reshape(height, scale.shape[1], -1)
        * scale.astype(jnp.float32)[:, :, None]
    )
    return (weight.astype(jnp.float32) + delta.reshape(weight.shape)).astype(jnp.bfloat16)


def body(
    tokens,
    route_ids,
    route_weight,
    gate_weight,
    up_weight,
    down_weight,
    gate_code,
    up_code,
    gate_scale,
    up_scale,
    down_code,
    down_scale,
):
    groups, share = lax.axis_size("group"), lax.axis_size("tp")
    group = lax.axis_index("group")
    rows, part = tokens.shape
    width = part * share
    depth = width // groups
    columns = down_code.shape[1]
    capacity = rows * route_ids.shape[1] * 5 // (EXPERTS * 4)
    expert = lax.axis_index("tp") // (share // EXPERTS)

    mine = lax.all_to_all(tokens, "tp", split_axis=0, concat_axis=1, tiled=True)
    mine = mine.reshape(rows // share, groups, depth).transpose(1, 0, 2)
    mine = lax.all_to_all(mine, "group", split_axis=0, concat_axis=0, tiled=True)
    every = lax.all_gather(mine, "tp", axis=1, tiled=True)

    combine = route_weight / jnp.sum(route_weight, axis=1, keepdims=True)
    named = route_ids == expert
    weight_row = jnp.sum(jnp.where(named, combine, jnp.zeros_like(combine)), axis=1)
    used = jnp.any(named, axis=1)
    place = jnp.cumsum(used.astype(jnp.int32)) - 1
    target = jnp.where(used, place, capacity)
    both = jnp.stack([target.astype(jnp.float32), weight_row], axis=0)
    both = lax.all_gather(both, "group", axis=0, tiled=False)
    target_all = both[:, 0].astype(jnp.int32)
    pick = target_all[:, None, :] == lax.broadcasted_iota(jnp.int32, (groups, capacity, rows), 1)
    slot_weight = jnp.sum(jnp.where(pick, both[:, 1][:, None, :], 0.0), axis=2)
    pick = pick.astype(jnp.bfloat16)

    picked = jnp.einsum("gsn,gnk->gsk", pick, every)
    picked = picked.reshape(groups * capacity, depth)

    gate_new = refresh_rows(
        lax.dynamic_slice_in_dim(gate_weight, group * depth, depth, 0), gate_code, gate_scale
    )
    up_new = refresh_rows(
        lax.dynamic_slice_in_dim(up_weight, group * depth, depth, 0), up_code, up_scale
    )
    down_new = refresh_cols(
        lax.dynamic_slice_in_dim(down_weight, group * columns, columns, 1), down_code, down_scale
    )
    both_new = jnp.concatenate([gate_new, up_new], axis=1)
    term = expert_terms(groups, picked, both_new, down_new, slot_weight.reshape(-1, 1))
    term = term.reshape(groups, capacity, columns)
    spread = jnp.einsum("gsn,gsk->gnk", pick, term)
    spread = spread.reshape(groups, share, rows // share, columns).transpose(1, 0, 2, 3)
    total = lax.psum_scatter(spread, "tp", scatter_dimension=0, tiled=True)[0]
    total = lax.all_to_all(total, "group", split_axis=0, concat_axis=0, tiled=True)
    total = total.transpose(1, 0, 2).reshape(rows // share, width)
    return lax.all_to_all(total, "tp", split_axis=1, concat_axis=0, tiled=True).astype(jnp.bfloat16)


def solution(mesh):
    placed = (
        P("group", "tp"),
        P("group", None),
        P("group", None),
        P(None, "tp"),
        P(None, "tp"),
        P("tp", None),
        P("group", "tp"),
        P("group", "tp"),
        P("group", "tp"),
        P("group", "tp"),
        P("tp", "group"),
        P("tp", "group"),
    )
    return jax.shard_map(
        body, mesh=mesh, in_specs=placed, out_specs=P("group", "tp"), check_vma=False
    )
```

```python
import functools

import jax
import jax.numpy as jnp
from jax import lax
from jax.experimental import pallas as pl
from jax.experimental.pallas import tpu as pltpu
from jax.sharding import PartitionSpec as P

EXPERTS = 4
CHUNK = 64


def expert_kernel(
    groups,
    chunk,
    x_ref,
    w_ref,
    down_ref,
    weight_ref,
    term_ref,
    out_up,
    out_low,
    in_up,
    in_low,
    hidden,
    sem,
):
    me = lax.axis_index("group")
    last = groups - 1
    half = x_ref.shape[0] // 2
    count = half // chunk
    width = w_ref.shape[1] // 2

    barrier = pltpu.get_barrier_semaphore()

    @pl.when(me > 0)
    def _():
        pl.semaphore_signal(
            barrier, inc=1, device_id={"group": me - 1}, device_id_type=pl.DeviceIdType.MESH
        )

    @pl.when(me < last)
    def _():
        pl.semaphore_signal(
            barrier, inc=1, device_id={"group": me + 1}, device_id_type=pl.DeviceIdType.MESH
        )

    @pl.when((me > 0) & (me < last))
    def _():
        pl.semaphore_wait(barrier, 2)

    @pl.when((me == 0) | (me == last))
    def _():
        pl.semaphore_wait(barrier, 1)

    def piece(k, start):
        return pl.ds(pl.multiple_of(start + k * chunk, chunk), chunk)

    def move(k, source, target, number, where):
        return pltpu.make_async_remote_copy(
            src_ref=source,
            dst_ref=target,
            send_sem=sem.at[number, k],
            recv_sem=sem.at[number + 1, k],
            device_id={"group": where},
            device_id_type=pl.DeviceIdType.MESH,
        )

    def sum_move(k, upward):
        if upward:
            return move(k, out_up.at[piece(k, 0)], in_up.at[piece(k, 0)], 0, lax.rem(me + 1, groups))
        return move(k, out_low.at[piece(k, 0)], in_low.at[piece(k, 0)], 2, lax.rem(me + last, groups))

    def hidden_move(k, upward):
        if upward:
            return move(k, hidden.at[piece(k, half)], hidden.at[piece(k, half)], 4, lax.rem(me + last, groups))
        return move(k, hidden.at[piece(k, 0)], hidden.at[piece(k, 0)], 6, lax.rem(me + 1, groups))

    def finish(k, start):
        rows = piece(k, start)
        term = jnp.dot(hidden[rows, :], down_ref[...], preferred_element_type=jnp.float32)
        term_ref[rows, :] = (term * weight_ref[rows, :]).astype(jnp.bfloat16)

    def add(k, upward):
        start = half if upward else 0
        first, final = (0, last) if upward else (last, 0)
        inside, outside = (in_up, out_up) if upward else (in_low, out_low)
        here = piece(k, 0)
        own = jnp.dot(x_ref[piece(k, start), :], w_ref[...], preferred_element_type=jnp.float32)

        @pl.when(me == first)
        def _():
            outside[here, :] = own.astype(jnp.bfloat16)

        @pl.when(me != first)
        def _():
            sum_move(k, upward).wait_recv()

            @pl.when(me != final)
            def _():
                outside[here, :] = (own + inside[here, :].astype(jnp.float32)).astype(jnp.bfloat16)

            @pl.when(me == final)
            def _():
                value = own + inside[here, :].astype(jnp.float32)
                gate, up = value[:, :width], value[:, width:]
                hidden[piece(k, start), :] = (gate / (1.0 + jnp.exp(-gate)) * up).astype(
                    jnp.bfloat16
                )

        @pl.when(me != final)
        def _():
            sum_move(k, upward).start()

        @pl.when(me == final)
        def _():
            hidden_move(k, upward).start()
            finish(k, start)

    def take(k, upward):
        final, end = (last, 0) if upward else (0, last)
        hidden_move(k, upward).wait_recv()

        @pl.when(me != end)
        def _():
            hidden_move(k, upward).start()

        finish(k, half if upward else 0)

    def step(t, _):
        for upward in (True, False):
            place = me if upward else last - me
            k = t - place

            @pl.when((k >= 0) & (k < count))
            def _():
                add(k, upward)

        for upward in (True, False):
            place = me if upward else last - me
            j = t - (2 * last - place)

            @pl.when((j >= 0) & (j < count) & (place != last))
            def _():
                take(j, upward)

        return 0

    lax.fori_loop(0, count + 2 * last, step, 0)

    def settle(k, _):
        for upward in (True, False):
            final, end = (last, 0) if upward else (0, last)

            @pl.when(me != final)
            def _():
                sum_move(k, upward).wait_send()

            @pl.when(me != end)
            def _():
                hidden_move(k, upward).wait_send()

        return 0

    lax.fori_loop(0, count, settle, 0)


def expert_terms(groups, picked, both_new, down_new, slot_weight):
    rows, columns = picked.shape[0], down_new.shape[1]
    half, width = rows // 2, down_new.shape[0]
    chunk = CHUNK
    vmem = pl.BlockSpec(memory_space=pltpu.VMEM)
    return pl.pallas_call(
        functools.partial(expert_kernel, groups, chunk),
        out_shape=jax.ShapeDtypeStruct((rows, columns), jnp.bfloat16),
        in_specs=[vmem] * 4,
        out_specs=vmem,
        scratch_shapes=[
            *[pltpu.VMEM((half, 2 * width), jnp.bfloat16)] * 4,
            pltpu.VMEM((rows, width), jnp.bfloat16),
            pltpu.SemaphoreType.DMA((8, half // chunk)),
        ],
        compiler_params=pltpu.CompilerParams(
            collective_id=0, has_side_effects=True, vmem_limit_bytes=48 * 1024 * 1024
        ),
    )(picked, both_new, down_new, slot_weight)


def refresh_rows(weight, code, scale):
    width = weight.shape[1]
    delta = (
        code.astype(jnp.float32).reshape(scale.shape[0], -1, width)
        * scale.astype(jnp.float32)[:, None, :]
    )
    return (weight.astype(jnp.float32) + delta.reshape(weight.shape)).astype(jnp.bfloat16)


def refresh_cols(weight, code, scale):
    height = weight.shape[0]
    delta = (
        code.astype(jnp.float32).reshape(height, scale.shape[1], -1)
        * scale.astype(jnp.float32)[:, :, None]
    )
    return (weight.astype(jnp.float32) + delta.reshape(weight.shape)).astype(jnp.bfloat16)


MESH = pl.DeviceIdType.MESH


def greet(groups, share, me, mine):
    barrier = pltpu.get_barrier_semaphore()
    for d in range(1, groups):
        where = lax.rem(me + d, groups)
        pl.semaphore_signal(barrier, inc=1, device_id={"group": where}, device_id_type=MESH)
    for e in range(1, share):
        where = lax.rem(mine + e, share)
        pl.semaphore_signal(barrier, inc=1, device_id={"tp": where}, device_id_type=MESH)
    pl.semaphore_wait(barrier, groups + share - 2)


def total_kernel(groups, share, bits, x_ref, out_ref, *scratch):
    me, mine = lax.axis_index("group"), lax.axis_index("tp")
    got = [scratch[2 * i : 2 * i + 2] for i in range(bits)]
    kept = [scratch[2 * (bits + i) : 2 * (bits + i) + 2] for i in range(bits - 1)]
    total, gathered, landed, sem, group_sem, plane_sem = scratch[2 * (2 * bits - 1) :]
    rows, columns = x_ref.shape[-2:]
    lane = columns // 2
    orders = [list(range(bits)), [0] + list(range(bits - 1, 0, -1))]
    part = out_ref.shape[1]
    ratio = columns // part

    greet(groups, share, me, mine)

    def digit(b):
        return lax.rem(mine // (1 << b), 2)

    def source(i, p, g, own):
        b = orders[p][i]
        left = sorted(set(range(bits)) - set(orders[p][:i]), reverse=True)
        wanted = digit(b) if own else 1 - digit(b)
        index = [g] + [wanted if other == b else slice(None) for other in left]
        if i == 0:
            return x_ref.at[tuple(index + [slice(None), pl.ds(p * lane, lane)])]
        return kept[i - 1][p].at[tuple(index)]

    def halving(i, p, g):
        b = orders[p][i]
        partner = mine + (1 << b) * (1 - 2 * digit(b))
        return pltpu.make_async_remote_copy(
            src_ref=source(i, p, g, False),
            dst_ref=got[i][p].at[g],
            send_sem=sem.at[0, i, p, g],
            recv_sem=sem.at[1, i, p, g],
            device_id={"tp": partner},
            device_id_type=MESH,
        )

    for g in range(groups):
        for p in range(2):
            halving(0, p, g).start()
    for i in range(bits):
        for g in range(groups):
            for p in range(2):
                halving(i, p, g).wait_recv()
                value = source(i, p, g, True)[...].astype(jnp.float32)
                value = (value + got[i][p][g].astype(jnp.float32)).astype(jnp.bfloat16)
                if i < bits - 1:
                    kept[i][p][g] = value
                    halving(i + 1, p, g).start()
                else:
                    total[g, :, p * lane : (p + 1) * lane] = value

    def to_group(d):
        where = lax.rem(me + d, groups)
        return pltpu.make_async_remote_copy(
            src_ref=total.at[where],
            dst_ref=gathered.at[me],
            send_sem=group_sem.at[0, d],
            recv_sem=group_sem.at[1, d],
            device_id={"group": where},
            device_id_type=MESH,
        )

    def from_group(d):
        where = lax.rem(me + groups - d, groups)
        return pltpu.make_async_remote_copy(
            src_ref=total.at[where],
            dst_ref=gathered.at[where],
            send_sem=group_sem.at[0, d],
            recv_sem=group_sem.at[1, d],
            device_id={"group": where},
            device_id_type=MESH,
        )

    def to_columns(where, slot, offset):
        return pltpu.make_async_remote_copy(
            src_ref=gathered.at[slot, :, pl.ds(offset, part)],
            dst_ref=landed.at[pl.ds(pl.multiple_of(mine * rows, rows), rows)],
            send_sem=plane_sem.at[0, where],
            recv_sem=plane_sem.at[1, mine],
            device_id={"tp": where},
            device_id_type=MESH,
        )

    for d in range(1, groups):
        to_group(d).start()
    gathered[me] = total[me]
    for d in range(groups):
        slot = lax.rem(me + groups - d, groups)
        if d > 0:
            from_group(d).wait_recv()
        for r in range(ratio):
            where = slot * ratio + r

            @pl.when(where != mine)
            def _():
                to_columns(where, slot, r * part).start()

            @pl.when(where == mine)
            def _():
                landed[pl.ds(pl.multiple_of(mine * rows, rows), rows), :] = gathered[
                    slot, :, r * part : (r + 1) * part
                ]

    def passed(where):
        return pltpu.make_async_remote_copy(
            src_ref=gathered.at[0, :, pl.ds(0, part)],
            dst_ref=landed.at[pl.ds(pl.multiple_of(where * rows, rows), rows)],
            send_sem=plane_sem.at[0, where],
            recv_sem=plane_sem.at[1, where],
            device_id={"tp": where},
            device_id_type=MESH,
        )

    for e in range(1, share):
        passed(lax.rem(mine + e, share)).wait_recv()
    out_ref[...] = landed[...]
    for e in range(1, share):
        where = lax.rem(mine + e, share)
        slot = where // ratio
        for r in range(ratio):

            @pl.when(lax.rem(where, ratio) == r)
            def _():
                to_columns(where, slot, r * part).wait_send()

    for d in range(1, groups):
        to_group(d).wait_send()
    for i in range(bits):
        for g in range(groups):
            for p in range(2):
                halving(i, p, g).wait_send()


def total_rows(groups, share, spread, part):
    rows, columns = spread.shape[1], spread.shape[2]
    bits = share.bit_length() - 1
    block = rows // share
    vmem = pl.BlockSpec(memory_space=pltpu.VMEM)
    sizes = [(groups,) + (2,) * (bits - 1 - i) + (block, columns // 2) for i in range(bits)]
    buffers = [pltpu.VMEM(size, jnp.bfloat16) for size in sizes for _ in range(2)]
    return pl.pallas_call(
        functools.partial(total_kernel, groups, share, bits),
        out_shape=jax.ShapeDtypeStruct((rows, part), jnp.bfloat16),
        in_specs=[vmem],
        out_specs=vmem,
        scratch_shapes=[
            *buffers,
            *buffers[:-2],
            pltpu.VMEM((groups, block, columns), jnp.bfloat16),
            pltpu.VMEM((groups, block, columns), jnp.bfloat16),
            pltpu.VMEM((rows, part), jnp.bfloat16),
            pltpu.SemaphoreType.DMA((2, bits, 2, groups)),
            pltpu.SemaphoreType.DMA((2, groups)),
            pltpu.SemaphoreType.DMA((2, share)),
        ],
        compiler_params=pltpu.CompilerParams(
            collective_id=1, has_side_effects=True, vmem_limit_bytes=48 * 1024 * 1024
        ),
    )(spread.reshape((groups,) + (2,) * bits + (block, columns)))


def body(
    tokens,
    route_ids,
    route_weight,
    gate_weight,
    up_weight,
    down_weight,
    gate_code,
    up_code,
    gate_scale,
    up_scale,
    down_code,
    down_scale,
):
    groups, share = lax.axis_size("group"), lax.axis_size("tp")
    group = lax.axis_index("group")
    rows, part = tokens.shape
    width = part * share
    depth = width // groups
    columns = down_code.shape[1]
    capacity = rows * route_ids.shape[1] * 5 // (EXPERTS * 4)
    expert = lax.axis_index("tp") // (share // EXPERTS)

    mine = lax.all_to_all(tokens, "tp", split_axis=0, concat_axis=1, tiled=True)
    mine = mine.reshape(rows // share, groups, depth).transpose(1, 0, 2)
    mine = lax.all_to_all(mine, "group", split_axis=0, concat_axis=0, tiled=True)
    every = lax.all_gather(mine, "tp", axis=1, tiled=True)

    combine = route_weight / jnp.sum(route_weight, axis=1, keepdims=True)
    named = route_ids == expert
    weight_row = jnp.sum(jnp.where(named, combine, jnp.zeros_like(combine)), axis=1)
    used = jnp.any(named, axis=1)
    place = jnp.cumsum(used.astype(jnp.int32)) - 1
    target = jnp.where(used, place, capacity)
    both = jnp.stack([target.astype(jnp.float32), weight_row], axis=0)
    both = lax.all_gather(both, "group", axis=0, tiled=False)
    target_all = both[:, 0].astype(jnp.int32)
    pick = target_all[:, None, :] == lax.broadcasted_iota(jnp.int32, (groups, capacity, rows), 1)
    slot_weight = jnp.sum(jnp.where(pick, both[:, 1][:, None, :], 0.0), axis=2)
    pick = pick.astype(jnp.bfloat16)

    picked = jnp.einsum("gsn,gnk->gsk", pick, every)
    picked = picked.reshape(groups * capacity, depth)

    gate_new = refresh_rows(
        lax.dynamic_slice_in_dim(gate_weight, group * depth, depth, 0), gate_code, gate_scale
    )
    up_new = refresh_rows(
        lax.dynamic_slice_in_dim(up_weight, group * depth, depth, 0), up_code, up_scale
    )
    down_new = refresh_cols(
        lax.dynamic_slice_in_dim(down_weight, group * columns, columns, 1), down_code, down_scale
    )
    both_new = jnp.concatenate([gate_new, up_new], axis=1)
    term = expert_terms(groups, picked, both_new, down_new, slot_weight.reshape(-1, 1))
    term = term.reshape(groups, capacity, columns)
    spread = jnp.einsum("gsn,gsk->gnk", pick, term)
    return total_rows(groups, share, spread, part)


def solution(mesh):
    placed = (
        P("group", "tp"),
        P("group", None),
        P("group", None),
        P(None, "tp"),
        P(None, "tp"),
        P("tp", None),
        P("group", "tp"),
        P("group", "tp"),
        P("group", "tp"),
        P("group", "tp"),
        P("tp", "group"),
        P("tp", "group"),
    )
    return jax.shard_map(
        body, mesh=mesh, in_specs=placed, out_specs=P("group", "tp"), check_vma=False
    )
```

```python
import functools

import jax
import jax.numpy as jnp
from jax import lax
from jax.experimental import pallas as pl
from jax.experimental.pallas import tpu as pltpu
from jax.sharding import PartitionSpec as P

EXPERTS = 4
CHUNK = 64


def expert_kernel(
    groups,
    chunk,
    x_ref,
    w_ref,
    down_ref,
    weight_ref,
    term_ref,
    out_up,
    out_low,
    in_up,
    in_low,
    hidden,
    sem,
):
    me = lax.axis_index("group")
    last = groups - 1
    half = x_ref.shape[0] // 2
    count = half // chunk
    width = w_ref.shape[1] // 2

    barrier = pltpu.get_barrier_semaphore()

    @pl.when(me > 0)
    def _():
        pl.semaphore_signal(
            barrier, inc=1, device_id={"group": me - 1}, device_id_type=pl.DeviceIdType.MESH
        )

    @pl.when(me < last)
    def _():
        pl.semaphore_signal(
            barrier, inc=1, device_id={"group": me + 1}, device_id_type=pl.DeviceIdType.MESH
        )

    @pl.when((me > 0) & (me < last))
    def _():
        pl.semaphore_wait(barrier, 2)

    @pl.when((me == 0) | (me == last))
    def _():
        pl.semaphore_wait(barrier, 1)

    def piece(k, start):
        return pl.ds(pl.multiple_of(start + k * chunk, chunk), chunk)

    def move(k, source, target, number, where):
        return pltpu.make_async_remote_copy(
            src_ref=source,
            dst_ref=target,
            send_sem=sem.at[number, k],
            recv_sem=sem.at[number + 1, k],
            device_id={"group": where},
            device_id_type=pl.DeviceIdType.MESH,
        )

    def sum_move(k, upward):
        if upward:
            return move(k, out_up.at[piece(k, 0)], in_up.at[piece(k, 0)], 0, lax.rem(me + 1, groups))
        return move(k, out_low.at[piece(k, 0)], in_low.at[piece(k, 0)], 2, lax.rem(me + last, groups))

    def hidden_move(k, upward):
        if upward:
            return move(k, hidden.at[piece(k, half)], hidden.at[piece(k, half)], 4, lax.rem(me + last, groups))
        return move(k, hidden.at[piece(k, 0)], hidden.at[piece(k, 0)], 6, lax.rem(me + 1, groups))

    def finish(k, start):
        rows = piece(k, start)
        term = jnp.dot(hidden[rows, :], down_ref[...], preferred_element_type=jnp.float32)
        term_ref[rows, :] = (term * weight_ref[rows, :]).astype(jnp.bfloat16)

    def add(k, upward):
        start = half if upward else 0
        first, final = (0, last) if upward else (last, 0)
        inside, outside = (in_up, out_up) if upward else (in_low, out_low)
        here = piece(k, 0)
        own = jnp.dot(x_ref[piece(k, start), :], w_ref[...], preferred_element_type=jnp.float32)

        @pl.when(me == first)
        def _():
            outside[here, :] = own.astype(jnp.bfloat16)

        @pl.when(me != first)
        def _():
            sum_move(k, upward).wait_recv()

            @pl.when(me != final)
            def _():
                outside[here, :] = (own + inside[here, :].astype(jnp.float32)).astype(jnp.bfloat16)

            @pl.when(me == final)
            def _():
                value = own + inside[here, :].astype(jnp.float32)
                gate, up = value[:, :width], value[:, width:]
                hidden[piece(k, start), :] = (gate / (1.0 + jnp.exp(-gate)) * up).astype(
                    jnp.bfloat16
                )

        @pl.when(me != final)
        def _():
            sum_move(k, upward).start()

        @pl.when(me == final)
        def _():
            hidden_move(k, upward).start()
            finish(k, start)

    def take(k, upward):
        final, end = (last, 0) if upward else (0, last)
        hidden_move(k, upward).wait_recv()

        @pl.when(me != end)
        def _():
            hidden_move(k, upward).start()

        finish(k, half if upward else 0)

    def step(t, _):
        for upward in (True, False):
            place = me if upward else last - me
            k = t - place

            @pl.when((k >= 0) & (k < count))
            def _():
                add(k, upward)

        for upward in (True, False):
            place = me if upward else last - me
            j = t - (2 * last - place)

            @pl.when((j >= 0) & (j < count) & (place != last))
            def _():
                take(j, upward)

        return 0

    lax.fori_loop(0, count + 2 * last, step, 0)

    def settle(k, _):
        for upward in (True, False):
            final, end = (last, 0) if upward else (0, last)

            @pl.when(me != final)
            def _():
                sum_move(k, upward).wait_send()

            @pl.when(me != end)
            def _():
                hidden_move(k, upward).wait_send()

        return 0

    lax.fori_loop(0, count, settle, 0)


def expert_terms(groups, picked, both_new, down_new, slot_weight):
    rows, columns = picked.shape[0], down_new.shape[1]
    half, width = rows // 2, down_new.shape[0]
    chunk = CHUNK
    vmem = pl.BlockSpec(memory_space=pltpu.VMEM)
    return pl.pallas_call(
        functools.partial(expert_kernel, groups, chunk),
        out_shape=jax.ShapeDtypeStruct((rows, columns), jnp.bfloat16),
        in_specs=[vmem] * 4,
        out_specs=vmem,
        scratch_shapes=[
            *[pltpu.VMEM((half, 2 * width), jnp.bfloat16)] * 4,
            pltpu.VMEM((rows, width), jnp.bfloat16),
            pltpu.SemaphoreType.DMA((8, half // chunk)),
        ],
        compiler_params=pltpu.CompilerParams(
            collective_id=0, has_side_effects=True, vmem_limit_bytes=48 * 1024 * 1024
        ),
    )(picked, both_new, down_new, slot_weight)


def refresh_rows(weight, code, scale):
    width = weight.shape[1]
    delta = (
        code.astype(jnp.float32).reshape(scale.shape[0], -1, width)
        * scale.astype(jnp.float32)[:, None, :]
    )
    return (weight.astype(jnp.float32) + delta.reshape(weight.shape)).astype(jnp.bfloat16)


def refresh_cols(weight, code, scale):
    height = weight.shape[0]
    delta = (
        code.astype(jnp.float32).reshape(height, scale.shape[1], -1)
        * scale.astype(jnp.float32)[:, :, None]
    )
    return (weight.astype(jnp.float32) + delta.reshape(weight.shape)).astype(jnp.bfloat16)


MESH = pl.DeviceIdType.MESH


def greet(groups, share, me, mine):
    barrier = pltpu.get_barrier_semaphore()
    for d in range(1, groups):
        where = lax.rem(me + d, groups)
        pl.semaphore_signal(barrier, inc=1, device_id={"group": where}, device_id_type=MESH)
    for e in range(1, share):
        where = lax.rem(mine + e, share)
        pl.semaphore_signal(barrier, inc=1, device_id={"tp": where}, device_id_type=MESH)
    pl.semaphore_wait(barrier, groups + share - 2)


def total_kernel(groups, share, bits, x_ref, out_ref, *scratch):
    me, mine = lax.axis_index("group"), lax.axis_index("tp")
    got = [scratch[2 * i : 2 * i + 2] for i in range(bits)]
    kept = [scratch[2 * (bits + i) : 2 * (bits + i) + 2] for i in range(bits - 1)]
    total, gathered, landed, sem, group_sem, plane_sem = scratch[2 * (2 * bits - 1) :]
    rows, columns = x_ref.shape[-2:]
    lane = columns // 2
    orders = [list(range(bits)), [0] + list(range(bits - 1, 0, -1))]
    part = out_ref.shape[1]
    ratio = columns // part

    greet(groups, share, me, mine)

    def digit(b):
        return lax.rem(mine // (1 << b), 2)

    def source(i, p, g, own):
        b = orders[p][i]
        left = sorted(set(range(bits)) - set(orders[p][:i]), reverse=True)
        wanted = digit(b) if own else 1 - digit(b)
        index = [g] + [wanted if other == b else slice(None) for other in left]
        if i == 0:
            return x_ref.at[tuple(index + [slice(None), pl.ds(p * lane, lane)])]
        return kept[i - 1][p].at[tuple(index)]

    def halving(i, p, g):
        b = orders[p][i]
        partner = mine + (1 << b) * (1 - 2 * digit(b))
        return pltpu.make_async_remote_copy(
            src_ref=source(i, p, g, False),
            dst_ref=got[i][p].at[g],
            send_sem=sem.at[0, i, p, g],
            recv_sem=sem.at[1, i, p, g],
            device_id={"tp": partner},
            device_id_type=MESH,
        )

    for g in range(groups):
        for p in range(2):
            halving(0, p, g).start()
    for i in range(bits):
        for g in range(groups):
            for p in range(2):
                halving(i, p, g).wait_recv()
                value = source(i, p, g, True)[...].astype(jnp.float32)
                value = (value + got[i][p][g].astype(jnp.float32)).astype(jnp.bfloat16)
                if i < bits - 1:
                    kept[i][p][g] = value
                    halving(i + 1, p, g).start()
                else:
                    total[g, :, p * lane : (p + 1) * lane] = value

    def to_group(d):
        where = lax.rem(me + d, groups)
        return pltpu.make_async_remote_copy(
            src_ref=total.at[where],
            dst_ref=gathered.at[me],
            send_sem=group_sem.at[0, d],
            recv_sem=group_sem.at[1, d],
            device_id={"group": where},
            device_id_type=MESH,
        )

    def from_group(d):
        where = lax.rem(me + groups - d, groups)
        return pltpu.make_async_remote_copy(
            src_ref=total.at[where],
            dst_ref=gathered.at[where],
            send_sem=group_sem.at[0, d],
            recv_sem=group_sem.at[1, d],
            device_id={"group": where},
            device_id_type=MESH,
        )

    def to_columns(where, slot, offset):
        return pltpu.make_async_remote_copy(
            src_ref=gathered.at[slot, :, pl.ds(offset, part)],
            dst_ref=landed.at[pl.ds(pl.multiple_of(mine * rows, rows), rows)],
            send_sem=plane_sem.at[0, where],
            recv_sem=plane_sem.at[1, mine],
            device_id={"tp": where},
            device_id_type=MESH,
        )

    for d in range(1, groups):
        to_group(d).start()
    gathered[me] = total[me]
    for d in range(groups):
        slot = lax.rem(me + groups - d, groups)
        if d > 0:
            from_group(d).wait_recv()
        for r in range(ratio):
            where = slot * ratio + r

            @pl.when(where != mine)
            def _():
                to_columns(where, slot, r * part).start()

            @pl.when(where == mine)
            def _():
                landed[pl.ds(pl.multiple_of(mine * rows, rows), rows), :] = gathered[
                    slot, :, r * part : (r + 1) * part
                ]

    def passed(where):
        return pltpu.make_async_remote_copy(
            src_ref=gathered.at[0, :, pl.ds(0, part)],
            dst_ref=landed.at[pl.ds(pl.multiple_of(where * rows, rows), rows)],
            send_sem=plane_sem.at[0, where],
            recv_sem=plane_sem.at[1, where],
            device_id={"tp": where},
            device_id_type=MESH,
        )

    for e in range(1, share):
        passed(lax.rem(mine + e, share)).wait_recv()
    out_ref[...] = landed[...]
    for e in range(1, share):
        where = lax.rem(mine + e, share)
        slot = where // ratio
        for r in range(ratio):

            @pl.when(lax.rem(where, ratio) == r)
            def _():
                to_columns(where, slot, r * part).wait_send()

    for d in range(1, groups):
        to_group(d).wait_send()
    for i in range(bits):
        for g in range(groups):
            for p in range(2):
                halving(i, p, g).wait_send()


def total_rows(groups, share, spread, part):
    rows, columns = spread.shape[1], spread.shape[2]
    bits = share.bit_length() - 1
    block = rows // share
    vmem = pl.BlockSpec(memory_space=pltpu.VMEM)
    sizes = [(groups,) + (2,) * (bits - 1 - i) + (block, columns // 2) for i in range(bits)]
    buffers = [pltpu.VMEM(size, jnp.bfloat16) for size in sizes for _ in range(2)]
    return pl.pallas_call(
        functools.partial(total_kernel, groups, share, bits),
        out_shape=jax.ShapeDtypeStruct((rows, part), jnp.bfloat16),
        in_specs=[vmem],
        out_specs=vmem,
        scratch_shapes=[
            *buffers,
            *buffers[:-2],
            pltpu.VMEM((groups, block, columns), jnp.bfloat16),
            pltpu.VMEM((groups, block, columns), jnp.bfloat16),
            pltpu.VMEM((rows, part), jnp.bfloat16),
            pltpu.SemaphoreType.DMA((2, bits, 2, groups)),
            pltpu.SemaphoreType.DMA((2, groups)),
            pltpu.SemaphoreType.DMA((2, share)),
        ],
        compiler_params=pltpu.CompilerParams(
            collective_id=1, has_side_effects=True, vmem_limit_bytes=48 * 1024 * 1024
        ),
    )(spread.reshape((groups,) + (2,) * bits + (block, columns)))


def pick_kernel(
    groups,
    share,
    bits,
    tokens_ref,
    route_ref,
    picked_ref,
    pick_ref,
    weight_ref,
    mid,
    every,
    table,
    table_sem,
    plane_sem,
    group_sem,
    sem,
):
    me, mine = lax.axis_index("group"), lax.axis_index("tp")
    rows, columns = mid.shape[1:]
    part = tokens_ref.shape[1]
    ratio = columns // part
    lane = columns // 2
    capacity = picked_ref.shape[1]
    orders = [list(range(bits - 1, -1, -1)), list(range(1, bits)) + [0]]

    greet(groups, share, me, mine)

    def digit(b):
        return lax.rem(mine // (1 << b), 2)

    def route(d, sending):
        slot = me if sending else lax.rem(me + groups - d, groups)
        where = lax.rem(me + d, groups)
        return pltpu.make_async_remote_copy(
            src_ref=route_ref,
            dst_ref=table.at[slot],
            send_sem=table_sem.at[0, d],
            recv_sem=table_sem.at[1, d],
            device_id={"group": where},
            device_id_type=MESH,
        )

    def block(where, slot, r, source):
        return pltpu.make_async_remote_copy(
            src_ref=tokens_ref.at[pl.ds(pl.multiple_of(where * rows, rows), rows)],
            dst_ref=mid.at[slot, :, pl.ds(r * part, part)],
            send_sem=plane_sem.at[0, where],
            recv_sem=plane_sem.at[1, source],
            device_id={"tp": where},
            device_id_type=MESH,
        )

    place = [digit(b) for b in range(bits - 1, -1, -1)]

    def slice_move(d, sending):
        where = lax.rem(me + d, groups)
        slot = me if sending else lax.rem(me + groups - d, groups)
        return pltpu.make_async_remote_copy(
            src_ref=mid.at[where],
            dst_ref=every.at[tuple([slot] + place)],
            send_sem=group_sem.at[0, d],
            recv_sem=group_sem.at[1, d],
            device_id={"group": where},
            device_id_type=MESH,
        )

    def doubling(i, p, d, sending):
        b = orders[p][i]
        done = orders[p][:i]
        slot = lax.rem(me + groups - d, groups)
        index = [slot]
        for other in range(bits - 1, -1, -1):
            if other in done:
                index.append(slice(None))
            elif other == b and not sending:
                index.append(1 - digit(other))
            else:
                index.append(digit(other))
        view = every.at[tuple(index + [slice(None), pl.ds(p * lane, lane)])]
        return pltpu.make_async_remote_copy(
            src_ref=view,
            dst_ref=view,
            send_sem=sem.at[0, i, p, d],
            recv_sem=sem.at[1, i, p, d],
            device_id={"tp": mine + (1 << b) * (1 - 2 * digit(b))},
            device_id_type=MESH,
        )

    def blocks(e, act):
        where = lax.rem(mine + e, share)
        for r in range(ratio):

            @pl.when(lax.rem(mine, ratio) == r)
            def _():
                act(block(where, mine // ratio, r, mine))

    for e in range(1, share):
        blocks(e, lambda copy: copy.start())
    for d in range(1, groups):
        route(d, True).start()
    for r in range(ratio):

        @pl.when(lax.rem(mine, ratio) == r)
        def _():
            mid[mine // ratio, :, r * part : (r + 1) * part] = tokens_ref[
                pl.ds(pl.multiple_of(mine * rows, rows), rows), :
            ]

    table[me] = route_ref[...]
    for d in list(range(1, groups)) + [0]:
        slot = lax.rem(me + d, groups)
        for r in range(ratio):
            origin = slot * ratio + r

            @pl.when(origin != mine)
            def _():
                block(origin, slot, r, origin).wait_recv()

        if d > 0:
            slice_move(d, True).start()
        else:
            every[tuple([me] + place)] = mid[me]

    for d in range(groups):
        if d > 0:
            slice_move(d, False).wait_recv()
        for p in range(2):
            doubling(0, p, d, True).start()
    for i in range(bits):
        for d in range(groups):
            for p in range(2):
                doubling(i, p, d, False).wait_recv()
                if i < bits - 1:
                    doubling(i + 1, p, d, True).start()
            if i == bits - 1:
                slot = lax.rem(me + groups - d, groups)
                if d > 0:
                    route(d, False).wait_recv()
                entry = table[slot]
                number = lax.broadcasted_iota(jnp.int32, (capacity, entry.shape[1]), 0)
                chosen = number.astype(jnp.float32) == entry[0:1, :]
                weight_ref[slot] = jnp.sum(
                    jnp.where(chosen, entry[1:2, :], 0.0), axis=1, keepdims=True
                )
                chosen = jnp.where(chosen, 1.0, 0.0).astype(jnp.bfloat16)
                pick_ref[slot] = chosen
                picked_ref[slot] = jnp.dot(
                    chosen,
                    every[slot].reshape(share * rows, columns),
                    preferred_element_type=jnp.float32,
                ).astype(jnp.bfloat16)

    for e in range(1, share):
        blocks(e, lambda copy: copy.wait_send())
    for d in range(1, groups):
        route(d, True).wait_send()
        slice_move(d, True).wait_send()
    for i in range(bits):
        for d in range(groups):
            for p in range(2):
                doubling(i, p, d, True).wait_send()


def pick_rows(groups, share, tokens, route, capacity):
    rows, part = tokens.shape
    columns = part * share // groups
    bits = share.bit_length() - 1
    block = rows // share
    vmem = pl.BlockSpec(memory_space=pltpu.VMEM)
    return pl.pallas_call(
        functools.partial(pick_kernel, groups, share, bits),
        out_shape=(
            jax.ShapeDtypeStruct((groups, capacity, columns), jnp.bfloat16),
            jax.ShapeDtypeStruct((groups, capacity, rows), jnp.bfloat16),
            jax.ShapeDtypeStruct((groups, capacity, 1), jnp.float32),
        ),
        in_specs=[vmem] * 2,
        out_specs=(vmem,) * 3,
        scratch_shapes=[
            pltpu.VMEM((groups, block, columns), jnp.bfloat16),
            pltpu.VMEM((groups,) + (2,) * bits + (block, columns), jnp.bfloat16),
            pltpu.VMEM((groups,) + route.shape, jnp.float32),
            pltpu.SemaphoreType.DMA((2, groups)),
            pltpu.SemaphoreType.DMA((2, share)),
            pltpu.SemaphoreType.DMA((2, groups)),
            pltpu.SemaphoreType.DMA((2, bits, 2, groups)),
        ],
        compiler_params=pltpu.CompilerParams(
            collective_id=2, has_side_effects=True, vmem_limit_bytes=48 * 1024 * 1024
        ),
    )(tokens, route)


def body(
    tokens,
    route_ids,
    route_weight,
    gate_weight,
    up_weight,
    down_weight,
    gate_code,
    up_code,
    gate_scale,
    up_scale,
    down_code,
    down_scale,
):
    groups, share = lax.axis_size("group"), lax.axis_size("tp")
    group = lax.axis_index("group")
    rows, part = tokens.shape
    width = part * share
    depth = width // groups
    columns = down_code.shape[1]
    capacity = rows * route_ids.shape[1] * 5 // (EXPERTS * 4)
    expert = lax.axis_index("tp") // (share // EXPERTS)

    combine = route_weight / jnp.sum(route_weight, axis=1, keepdims=True)
    named = route_ids == expert
    weight_row = jnp.sum(jnp.where(named, combine, jnp.zeros_like(combine)), axis=1)
    used = jnp.any(named, axis=1)
    place = jnp.cumsum(used.astype(jnp.int32)) - 1
    target = jnp.where(used, place, capacity)
    route = jnp.stack([target.astype(jnp.float32), weight_row], axis=0)
    route = jnp.pad(route, ((0, 6), (0, 0)))
    picked, pick, slot_weight = pick_rows(groups, share, tokens, route, capacity)
    picked = picked.reshape(groups * capacity, depth)

    gate_new = refresh_rows(
        lax.dynamic_slice_in_dim(gate_weight, group * depth, depth, 0), gate_code, gate_scale
    )
    up_new = refresh_rows(
        lax.dynamic_slice_in_dim(up_weight, group * depth, depth, 0), up_code, up_scale
    )
    down_new = refresh_cols(
        lax.dynamic_slice_in_dim(down_weight, group * columns, columns, 1), down_code, down_scale
    )
    both_new = jnp.concatenate([gate_new, up_new], axis=1)
    term = expert_terms(groups, picked, both_new, down_new, slot_weight.reshape(-1, 1))
    term = term.reshape(groups, capacity, columns)
    spread = jnp.einsum("gsn,gsk->gnk", pick, term)
    return total_rows(groups, share, spread, part)


def solution(mesh):
    placed = (
        P("group", "tp"),
        P("group", None),
        P("group", None),
        P(None, "tp"),
        P(None, "tp"),
        P("tp", None),
        P("group", "tp"),
        P("group", "tp"),
        P("group", "tp"),
        P("group", "tp"),
        P("tp", "group"),
        P("tp", "group"),
    )
    return jax.shard_map(
        body, mesh=mesh, in_specs=placed, out_specs=P("group", "tp"), check_vma=False
    )
```

```python
import functools

import jax
import jax.numpy as jnp
from jax import lax
from jax.experimental import pallas as pl
from jax.experimental.pallas import tpu as pltpu
from jax.sharding import PartitionSpec as P

EXPERTS = 4
CHUNK = 64


def expert_kernel(
    groups,
    chunk,
    x_ref,
    w_ref,
    down_ref,
    weight_ref,
    term_ref,
    out_up,
    out_low,
    in_up,
    in_low,
    hidden,
    ahead,
    sem,
):
    me = lax.axis_index("group")
    last = groups - 1
    half = x_ref.shape[0] // 2
    count = half // chunk
    width = w_ref.shape[1] // 2

    barrier = pltpu.get_barrier_semaphore()

    @pl.when(me > 0)
    def _():
        pl.semaphore_signal(
            barrier, inc=1, device_id={"group": me - 1}, device_id_type=pl.DeviceIdType.MESH
        )

    @pl.when(me < last)
    def _():
        pl.semaphore_signal(
            barrier, inc=1, device_id={"group": me + 1}, device_id_type=pl.DeviceIdType.MESH
        )

    @pl.when((me > 0) & (me < last))
    def _():
        pl.semaphore_wait(barrier, 2)

    @pl.when((me == 0) | (me == last))
    def _():
        pl.semaphore_wait(barrier, 1)

    def piece(k, start):
        return pl.ds(pl.multiple_of(start + k * chunk, chunk), chunk)

    def move(k, source, target, number, where):
        return pltpu.make_async_remote_copy(
            src_ref=source,
            dst_ref=target,
            send_sem=sem.at[number, k],
            recv_sem=sem.at[number + 1, k],
            device_id={"group": where},
            device_id_type=pl.DeviceIdType.MESH,
        )

    def sum_move(k, upward):
        if upward:
            return move(k, out_up.at[piece(k, 0)], in_up.at[piece(k, 0)], 0, lax.rem(me + 1, groups))
        return move(k, out_low.at[piece(k, 0)], in_low.at[piece(k, 0)], 2, lax.rem(me + last, groups))

    def hidden_move(k, upward):
        if upward:
            return move(k, hidden.at[piece(k, half)], hidden.at[piece(k, half)], 4, lax.rem(me + last, groups))
        return move(k, hidden.at[piece(k, 0)], hidden.at[piece(k, 0)], 6, lax.rem(me + 1, groups))

    def finish(k, start):
        rows = piece(k, start)
        term = jnp.dot(hidden[rows, :], down_ref[...], preferred_element_type=jnp.float32)
        term_ref[rows, :] = (term * weight_ref[rows, :]).astype(jnp.bfloat16)

    def add(k, upward):
        start = half if upward else 0
        first, final = (0, last) if upward else (last, 0)
        inside, outside = (in_up, out_up) if upward else (in_low, out_low)
        here = piece(k, 0)
        own = ahead[int(upward)]

        @pl.when(me == first)
        def _():
            outside[here, :] = own.astype(jnp.bfloat16)

        @pl.when(me != first)
        def _():
            sum_move(k, upward).wait_recv()

            @pl.when(me != final)
            def _():
                outside[here, :] = (own + inside[here, :].astype(jnp.float32)).astype(jnp.bfloat16)

            @pl.when(me == final)
            def _():
                value = own + inside[here, :].astype(jnp.float32)
                gate, up = value[:, :width], value[:, width:]
                hidden[piece(k, start), :] = (gate / (1.0 + jnp.exp(-gate)) * up).astype(
                    jnp.bfloat16
                )

        @pl.when(me != final)
        def _():
            sum_move(k, upward).start()

        @pl.when(me == final)
        def _():
            hidden_move(k, upward).start()

    def prepare(t):
        for upward in (True, False):
            k = t - (me if upward else last - me)

            @pl.when((k >= 0) & (k < count))
            def _():
                ahead[int(upward)] = jnp.dot(
                    x_ref[piece(k, half if upward else 0), :],
                    w_ref[...],
                    preferred_element_type=jnp.float32,
                )

    def take(k, upward):
        final, end = (last, 0) if upward else (0, last)
        hidden_move(k, upward).wait_recv()

        @pl.when(me != end)
        def _():
            hidden_move(k, upward).start()

    def step(t, _):
        for upward in (True, False):
            place = me if upward else last - me
            k = t - place

            @pl.when((k >= 0) & (k < count))
            def _():
                add(k, upward)

        prepare(t + 1)
        for upward in (True, False):
            place = me if upward else last - me
            k = t - place
            j = k - 1 - 2 * (last - place)
            k = jnp.where(place == last, k, j)

            @pl.when((k >= 0) & (k < count))
            def _():
                finish(k, half if upward else 0)

        for upward in (True, False):
            place = me if upward else last - me
            j = t - (2 * last - place)

            @pl.when((j >= 0) & (j < count) & (place != last))
            def _():
                take(j, upward)

        return 0

    prepare(0)
    lax.fori_loop(0, count + 2 * last + 1, step, 0)

    def settle(k, _):
        for upward in (True, False):
            final, end = (last, 0) if upward else (0, last)

            @pl.when(me != final)
            def _():
                sum_move(k, upward).wait_send()

            @pl.when(me != end)
            def _():
                hidden_move(k, upward).wait_send()

        return 0

    lax.fori_loop(0, count, settle, 0)


def expert_terms(groups, picked, both_new, down_new, slot_weight):
    rows, columns = picked.shape[0], down_new.shape[1]
    half, width = rows // 2, down_new.shape[0]
    chunk = CHUNK
    vmem = pl.BlockSpec(memory_space=pltpu.VMEM)
    return pl.pallas_call(
        functools.partial(expert_kernel, groups, chunk),
        out_shape=jax.ShapeDtypeStruct((rows, columns), jnp.bfloat16),
        in_specs=[vmem] * 4,
        out_specs=vmem,
        scratch_shapes=[
            *[pltpu.VMEM((half, 2 * width), jnp.bfloat16)] * 4,
            pltpu.VMEM((rows, width), jnp.bfloat16),
            pltpu.VMEM((2, chunk, 2 * width), jnp.float32),
            pltpu.SemaphoreType.DMA((8, half // chunk)),
        ],
        compiler_params=pltpu.CompilerParams(
            collective_id=0, has_side_effects=True, vmem_limit_bytes=48 * 1024 * 1024
        ),
    )(picked, both_new, down_new, slot_weight)


def refresh_rows(weight, code, scale):
    width = weight.shape[1]
    delta = (
        code.astype(jnp.float32).reshape(scale.shape[0], -1, width)
        * scale.astype(jnp.float32)[:, None, :]
    )
    return (weight.astype(jnp.float32) + delta.reshape(weight.shape)).astype(jnp.bfloat16)


def refresh_cols(weight, code, scale):
    height = weight.shape[0]
    delta = (
        code.astype(jnp.float32).reshape(height, scale.shape[1], -1)
        * scale.astype(jnp.float32)[:, :, None]
    )
    return (weight.astype(jnp.float32) + delta.reshape(weight.shape)).astype(jnp.bfloat16)


MESH = pl.DeviceIdType.MESH


def greet(groups, share, me, mine):
    barrier = pltpu.get_barrier_semaphore()
    for d in range(1, groups):
        where = lax.rem(me + d, groups)
        pl.semaphore_signal(barrier, inc=1, device_id={"group": where}, device_id_type=MESH)
    for e in range(1, share):
        where = lax.rem(mine + e, share)
        pl.semaphore_signal(barrier, inc=1, device_id={"tp": where}, device_id_type=MESH)
    pl.semaphore_wait(barrier, groups + share - 2)


def total_kernel(groups, share, bits, x_ref, out_ref, *scratch):
    me, mine = lax.axis_index("group"), lax.axis_index("tp")
    got = [scratch[2 * i : 2 * i + 2] for i in range(bits)]
    kept = [scratch[2 * (bits + i) : 2 * (bits + i) + 2] for i in range(bits - 1)]
    total, gathered, landed, sem, group_sem, plane_sem = scratch[2 * (2 * bits - 1) :]
    rows, columns = x_ref.shape[-2:]
    lane = columns // 2
    orders = [list(range(bits)), [0] + list(range(bits - 1, 0, -1))]
    part = out_ref.shape[1]
    ratio = columns // part

    greet(groups, share, me, mine)

    def digit(b):
        return lax.rem(mine // (1 << b), 2)

    def source(i, p, g, own):
        b = orders[p][i]
        left = sorted(set(range(bits)) - set(orders[p][:i]), reverse=True)
        wanted = digit(b) if own else 1 - digit(b)
        index = [g] + [wanted if other == b else slice(None) for other in left]
        if i == 0:
            return x_ref.at[tuple(index + [slice(None), pl.ds(p * lane, lane)])]
        return kept[i - 1][p].at[tuple(index)]

    def halving(i, p, g):
        b = orders[p][i]
        partner = mine + (1 << b) * (1 - 2 * digit(b))
        return pltpu.make_async_remote_copy(
            src_ref=source(i, p, g, False),
            dst_ref=got[i][p].at[g],
            send_sem=sem.at[0, i, p, g],
            recv_sem=sem.at[1, i, p, g],
            device_id={"tp": partner},
            device_id_type=MESH,
        )

    for g in range(groups):
        for p in range(2):
            halving(0, p, g).start()
    for i in range(bits):
        for g in range(groups):
            for p in range(2):
                halving(i, p, g).wait_recv()
                value = source(i, p, g, True)[...].astype(jnp.float32)
                value = (value + got[i][p][g].astype(jnp.float32)).astype(jnp.bfloat16)
                if i < bits - 1:
                    kept[i][p][g] = value
                    halving(i + 1, p, g).start()
                else:
                    total[g, :, p * lane : (p + 1) * lane] = value

    def to_group(d):
        where = lax.rem(me + d, groups)
        return pltpu.make_async_remote_copy(
            src_ref=total.at[where],
            dst_ref=gathered.at[me],
            send_sem=group_sem.at[0, d],
            recv_sem=group_sem.at[1, d],
            device_id={"group": where},
            device_id_type=MESH,
        )

    def from_group(d):
        where = lax.rem(me + groups - d, groups)
        return pltpu.make_async_remote_copy(
            src_ref=total.at[where],
            dst_ref=gathered.at[where],
            send_sem=group_sem.at[0, d],
            recv_sem=group_sem.at[1, d],
            device_id={"group": where},
            device_id_type=MESH,
        )

    def to_columns(where, slot, offset):
        return pltpu.make_async_remote_copy(
            src_ref=gathered.at[slot, :, pl.ds(offset, part)],
            dst_ref=landed.at[pl.ds(pl.multiple_of(mine * rows, rows), rows)],
            send_sem=plane_sem.at[0, where],
            recv_sem=plane_sem.at[1, mine],
            device_id={"tp": where},
            device_id_type=MESH,
        )

    for d in range(1, groups):
        to_group(d).start()
    gathered[me] = total[me]
    for d in range(groups):
        slot = lax.rem(me + groups - d, groups)
        if d > 0:
            from_group(d).wait_recv()
        for r in range(ratio):
            where = slot * ratio + r

            @pl.when(where != mine)
            def _():
                to_columns(where, slot, r * part).start()

            @pl.when(where == mine)
            def _():
                landed[pl.ds(pl.multiple_of(mine * rows, rows), rows), :] = gathered[
                    slot, :, r * part : (r + 1) * part
                ]

    def passed(where):
        return pltpu.make_async_remote_copy(
            src_ref=gathered.at[0, :, pl.ds(0, part)],
            dst_ref=landed.at[pl.ds(pl.multiple_of(where * rows, rows), rows)],
            send_sem=plane_sem.at[0, where],
            recv_sem=plane_sem.at[1, where],
            device_id={"tp": where},
            device_id_type=MESH,
        )

    for e in range(1, share):
        passed(lax.rem(mine + e, share)).wait_recv()
    out_ref[...] = landed[...]
    for e in range(1, share):
        where = lax.rem(mine + e, share)
        slot = where // ratio
        for r in range(ratio):

            @pl.when(lax.rem(where, ratio) == r)
            def _():
                to_columns(where, slot, r * part).wait_send()

    for d in range(1, groups):
        to_group(d).wait_send()
    for i in range(bits):
        for g in range(groups):
            for p in range(2):
                halving(i, p, g).wait_send()


def total_rows(groups, share, spread, part):
    rows, columns = spread.shape[1], spread.shape[2]
    bits = share.bit_length() - 1
    block = rows // share
    vmem = pl.BlockSpec(memory_space=pltpu.VMEM)
    sizes = [(groups,) + (2,) * (bits - 1 - i) + (block, columns // 2) for i in range(bits)]
    buffers = [pltpu.VMEM(size, jnp.bfloat16) for size in sizes for _ in range(2)]
    return pl.pallas_call(
        functools.partial(total_kernel, groups, share, bits),
        out_shape=jax.ShapeDtypeStruct((rows, part), jnp.bfloat16),
        in_specs=[vmem],
        out_specs=vmem,
        scratch_shapes=[
            *buffers,
            *buffers[:-2],
            pltpu.VMEM((groups, block, columns), jnp.bfloat16),
            pltpu.VMEM((groups, block, columns), jnp.bfloat16),
            pltpu.VMEM((rows, part), jnp.bfloat16),
            pltpu.SemaphoreType.DMA((2, bits, 2, groups)),
            pltpu.SemaphoreType.DMA((2, groups)),
            pltpu.SemaphoreType.DMA((2, share)),
        ],
        compiler_params=pltpu.CompilerParams(
            collective_id=1, has_side_effects=True, vmem_limit_bytes=48 * 1024 * 1024
        ),
    )(spread.reshape((groups,) + (2,) * bits + (block, columns)))


def pick_kernel(
    groups,
    share,
    bits,
    tokens_ref,
    route_ref,
    picked_ref,
    pick_ref,
    weight_ref,
    mid,
    every,
    table,
    table_sem,
    plane_sem,
    group_sem,
    sem,
):
    me, mine = lax.axis_index("group"), lax.axis_index("tp")
    rows, columns = mid.shape[1:]
    part = tokens_ref.shape[1]
    ratio = columns // part
    lane = columns // 2
    capacity = picked_ref.shape[1]
    orders = [list(range(bits - 1, -1, -1)), list(range(1, bits)) + [0]]

    greet(groups, share, me, mine)

    def digit(b):
        return lax.rem(mine // (1 << b), 2)

    def route(d, sending):
        slot = me if sending else lax.rem(me + groups - d, groups)
        where = lax.rem(me + d, groups)
        return pltpu.make_async_remote_copy(
            src_ref=route_ref,
            dst_ref=table.at[slot],
            send_sem=table_sem.at[0, d],
            recv_sem=table_sem.at[1, d],
            device_id={"group": where},
            device_id_type=MESH,
        )

    def block(where, slot, r, source):
        return pltpu.make_async_remote_copy(
            src_ref=tokens_ref.at[pl.ds(pl.multiple_of(where * rows, rows), rows)],
            dst_ref=mid.at[slot, :, pl.ds(r * part, part)],
            send_sem=plane_sem.at[0, where],
            recv_sem=plane_sem.at[1, source],
            device_id={"tp": where},
            device_id_type=MESH,
        )

    place = [digit(b) for b in range(bits - 1, -1, -1)]

    def slice_move(d, sending):
        where = lax.rem(me + d, groups)
        slot = me if sending else lax.rem(me + groups - d, groups)
        return pltpu.make_async_remote_copy(
            src_ref=mid.at[where],
            dst_ref=every.at[tuple([slot] + place)],
            send_sem=group_sem.at[0, d],
            recv_sem=group_sem.at[1, d],
            device_id={"group": where},
            device_id_type=MESH,
        )

    def doubling(i, p, d, sending):
        b = orders[p][i]
        done = orders[p][:i]
        slot = lax.rem(me + groups - d, groups)
        index = [slot]
        for other in range(bits - 1, -1, -1):
            if other in done:
                index.append(slice(None))
            elif other == b and not sending:
                index.append(1 - digit(other))
            else:
                index.append(digit(other))
        view = every.at[tuple(index + [slice(None), pl.ds(p * lane, lane)])]
        return pltpu.make_async_remote_copy(
            src_ref=view,
            dst_ref=view,
            send_sem=sem.at[0, i, p, d],
            recv_sem=sem.at[1, i, p, d],
            device_id={"tp": mine + (1 << b) * (1 - 2 * digit(b))},
            device_id_type=MESH,
        )

    def blocks(e, act):
        where = lax.rem(mine + e, share)
        for r in range(ratio):

            @pl.when(lax.rem(mine, ratio) == r)
            def _():
                act(block(where, mine // ratio, r, mine))

    for e in range(1, share):
        blocks(e, lambda copy: copy.start())
    for d in range(1, groups):
        route(d, True).start()
    for r in range(ratio):

        @pl.when(lax.rem(mine, ratio) == r)
        def _():
            mid[mine // ratio, :, r * part : (r + 1) * part] = tokens_ref[
                pl.ds(pl.multiple_of(mine * rows, rows), rows), :
            ]

    table[me] = route_ref[...]
    for d in list(range(1, groups)) + [0]:
        slot = lax.rem(me + d, groups)
        for r in range(ratio):
            origin = slot * ratio + r

            @pl.when(origin != mine)
            def _():
                block(origin, slot, r, origin).wait_recv()

        if d > 0:
            slice_move(d, True).start()
        else:
            every[tuple([me] + place)] = mid[me]

    for d in range(groups):
        if d > 0:
            slice_move(d, False).wait_recv()
        for p in range(2):
            doubling(0, p, d, True).start()
    for i in range(bits):
        for d in range(groups):
            for p in range(2):
                doubling(i, p, d, False).wait_recv()
                if i < bits - 1:
                    doubling(i + 1, p, d, True).start()
            if i == bits - 1:
                slot = lax.rem(me + groups - d, groups)
                if d > 0:
                    route(d, False).wait_recv()
                entry = table[slot]
                number = lax.broadcasted_iota(jnp.int32, (capacity, entry.shape[1]), 0)
                chosen = number.astype(jnp.float32) == entry[0:1, :]
                weight_ref[slot] = jnp.sum(
                    jnp.where(chosen, entry[1:2, :], 0.0), axis=1, keepdims=True
                )
                chosen = jnp.where(chosen, 1.0, 0.0).astype(jnp.bfloat16)
                pick_ref[slot] = chosen
                picked_ref[slot] = jnp.dot(
                    chosen,
                    every[slot].reshape(share * rows, columns),
                    preferred_element_type=jnp.float32,
                ).astype(jnp.bfloat16)

    for e in range(1, share):
        blocks(e, lambda copy: copy.wait_send())
    for d in range(1, groups):
        route(d, True).wait_send()
        slice_move(d, True).wait_send()
    for i in range(bits):
        for d in range(groups):
            for p in range(2):
                doubling(i, p, d, True).wait_send()


def pick_rows(groups, share, tokens, route, capacity):
    rows, part = tokens.shape
    columns = part * share // groups
    bits = share.bit_length() - 1
    block = rows // share
    vmem = pl.BlockSpec(memory_space=pltpu.VMEM)
    return pl.pallas_call(
        functools.partial(pick_kernel, groups, share, bits),
        out_shape=(
            jax.ShapeDtypeStruct((groups, capacity, columns), jnp.bfloat16),
            jax.ShapeDtypeStruct((groups, capacity, rows), jnp.bfloat16),
            jax.ShapeDtypeStruct((groups, capacity, 1), jnp.float32),
        ),
        in_specs=[vmem] * 2,
        out_specs=(vmem,) * 3,
        scratch_shapes=[
            pltpu.VMEM((groups, block, columns), jnp.bfloat16),
            pltpu.VMEM((groups,) + (2,) * bits + (block, columns), jnp.bfloat16),
            pltpu.VMEM((groups,) + route.shape, jnp.float32),
            pltpu.SemaphoreType.DMA((2, groups)),
            pltpu.SemaphoreType.DMA((2, share)),
            pltpu.SemaphoreType.DMA((2, groups)),
            pltpu.SemaphoreType.DMA((2, bits, 2, groups)),
        ],
        compiler_params=pltpu.CompilerParams(
            collective_id=2, has_side_effects=True, vmem_limit_bytes=48 * 1024 * 1024
        ),
    )(tokens, route)


def body(
    tokens,
    route_ids,
    route_weight,
    gate_weight,
    up_weight,
    down_weight,
    gate_code,
    up_code,
    gate_scale,
    up_scale,
    down_code,
    down_scale,
):
    groups, share = lax.axis_size("group"), lax.axis_size("tp")
    group = lax.axis_index("group")
    rows, part = tokens.shape
    width = part * share
    depth = width // groups
    columns = down_code.shape[1]
    capacity = rows * route_ids.shape[1] * 5 // (EXPERTS * 4)
    expert = lax.axis_index("tp") // (share // EXPERTS)

    combine = route_weight / jnp.sum(route_weight, axis=1, keepdims=True)
    named = route_ids == expert
    weight_row = jnp.sum(jnp.where(named, combine, jnp.zeros_like(combine)), axis=1)
    used = jnp.any(named, axis=1)
    place = jnp.cumsum(used.astype(jnp.int32)) - 1
    target = jnp.where(used, place, capacity)
    route = jnp.stack([target.astype(jnp.float32), weight_row], axis=0)
    route = jnp.pad(route, ((0, 6), (0, 0)))
    picked, pick, slot_weight = pick_rows(groups, share, tokens, route, capacity)
    picked = picked.reshape(groups * capacity, depth)

    gate_new = refresh_rows(
        lax.dynamic_slice_in_dim(gate_weight, group * depth, depth, 0), gate_code, gate_scale
    )
    up_new = refresh_rows(
        lax.dynamic_slice_in_dim(up_weight, group * depth, depth, 0), up_code, up_scale
    )
    down_new = refresh_cols(
        lax.dynamic_slice_in_dim(down_weight, group * columns, columns, 1), down_code, down_scale
    )
    both_new = jnp.concatenate([gate_new, up_new], axis=1)
    term = expert_terms(groups, picked, both_new, down_new, slot_weight.reshape(-1, 1))
    term = term.reshape(groups, capacity, columns)
    spread = jnp.einsum("gsn,gsk->gnk", pick, term)
    return total_rows(groups, share, spread, part)


def solution(mesh):
    placed = (
        P("group", "tp"),
        P("group", None),
        P("group", None),
        P(None, "tp"),
        P(None, "tp"),
        P("tp", None),
        P("group", "tp"),
        P("group", "tp"),
        P("group", "tp"),
        P("group", "tp"),
        P("tp", "group"),
        P("tp", "group"),
    )
    return jax.shard_map(
        body, mesh=mesh, in_specs=placed, out_specs=P("group", "tp"), check_vma=False
    )
```
